128 devices in a mesh: slab: 8 (over y, core), col: 16 (over x, z).
Axes of the slice: x: 4, y: 4, z: 4, core: 2. Of those that a mesh axis runs over, the one named last changes fastest.
Arguments:
- level_set: float32 [8, 16, 12, 16, 4096], P('slab', 'col'), may hold values from -6 to 6
- active: int32 [8, 16, 12], P('slab', 'col'), may hold values from 0 to 1, as said below
- destination: int32 [8, 16, 12], P('slab', 'col'), may hold values from -1 to 95, as said below
Outputs:
- relaxed: float32 [8, 16, 6, 16, 4096], P('slab', 'col')
The draws below stay inside these ranges and needn't reach their ends.
Inputs may be any that keep to these rules, and one draw needn't show every extreme that they name: `active`: along col, 4 devices of each slab have 6 + 6 live bricks and the others between 1 and 2. `destination`: -1 exactly where active is 0. The places of one slab are distinct. A device keeps its first 6 live bricks, in order of position, in its own slots 0 to 5 when it has more than that, and all of them otherwise; a device sends at most one brick to each other device, and at least one device in each slab sends one to 6 devices and fills all 6 slots.
All inputs are finite; a program needn't handle non-finite values.
Results may differ from the reference program's by a relative error of at most 0.0003.
Values sent between devices are 32-bit elements; how exact they have to be, the bound alone decides.
A program may use at most 128 MiB of HBM per device.

```python
import jax
import jax.numpy as jnp
from jax import lax

BZ = 16
BY = 64
BX = 64
RX = 12
STEPS = 1
W = 6
OVER = 6
N_SLAB = 8
N_COL = 16


def band_plan(key):

    def slab_plan(slab_key):
        role_key, count_key, place_key = jax.random.split(slab_key, 3)
        heavy_total = N_COL // 4
        light_total = N_COL - heavy_total
        role_of_col = jax.random.permutation(role_key, N_COL).astype(jnp.int32)
        col_of_role = jnp.argsort(role_of_col).astype(jnp.int32)
        light_live = jax.random.randint(count_key, (N_COL,), 1, W - heavy_total + 1, dtype=jnp.int32)
        is_heavy = role_of_col < heavy_total
        live_count = jnp.where(is_heavy, W + OVER, light_live).astype(jnp.int32)
        position_rank = jax.vmap(lambda member: jax.random.permutation(member, RX))(jax.random.split(place_key, N_COL)).astype(jnp.int32)
        is_live = (position_rank < live_count[:, None]).astype(jnp.int32)
        order_index = jnp.cumsum(is_live, axis=1) - is_live
        spill_index = order_index - W
        light_role = (role_of_col[:, None] * OVER + spill_index) % light_total
        earlier = jnp.arange(heavy_total, dtype=jnp.int32)
        covers = (light_role[:, :, None] - earlier[None, None, :] * OVER) % light_total < OVER
        arrival_rank = jnp.sum(covers & (earlier[None, None, :] < role_of_col[:, None, None]), axis=2).astype(jnp.int32)
        receiver = col_of_role[heavy_total + light_role]
        received_slot = live_count[receiver] + arrival_rank
        col_ids = jnp.arange(N_COL, dtype=jnp.int32)[:, None]
        stays_home = jnp.logical_not(is_heavy)[:, None] | (order_index < W)
        target = jnp.where(stays_home, col_ids * W + order_index, receiver * W + received_slot)
        target = jnp.where(is_live > 0, target, -1)
        return (is_live.astype(jnp.int32), target.astype(jnp.int32))
    return jax.vmap(slab_plan)(jax.random.split(key, N_SLAB))


def draw_active(key, part):
    return band_plan(key)[0]


def draw_destination(key, part):
    return band_plan(key)[1]


def shard_levels(own_key, shape, cuts, low, top_value):
    def one(dim, blocks):
        steps = jax.random.uniform(jax.random.fold_in(jax.random.fold_in(own_key, 6), dim), (blocks,), jnp.float32, low / len(cuts), top_value / len(cuts))
        return jnp.repeat(jnp.exp(steps), shape[dim] // blocks).reshape((-1,) + (1,) * (len(shape) - dim - 1))

    loudness = one(*cuts[0])
    for cut in cuts[1:]:
        loudness = loudness * one(*cut)
    return loudness


def bell_draw(rng, shape, spread, most, shards=(), kind=jnp.bfloat16):
    values = jax.random.normal(rng, shape, jnp.float32) * spread
    if len(shards) > 0:
        values = shard_levels(rng, shape, shards, -0.22, 0.18) * values
    return jnp.clip(values, min=-most, max=most).astype(kind)


def setup_inputs(seed: int = 0) -> dict:
    key_list = jax.random.split(jax.random.key(seed), 4)
    level_set = bell_draw(key_list[0], (N_SLAB, N_COL, RX, BZ, BY * BX), 1.0, 6.0, ((0, 8), (1, 16)), jnp.float32)
    active = draw_active(jax.random.fold_in(key_list[3], 71), 0)
    destination = draw_destination(jax.random.fold_in(key_list[3], 71), 0)
    return dict(level_set=level_set, active=active, destination=destination)


WENO_EPSILON = 1e-06
TIME_STEP = 0.3

def weno_blend(left_far, left_near, centre, right_near, right_far):
    part_one = (2.0 * left_far - 7.0 * left_near + 11.0 * centre) / 6.0
    part_two = (-left_near + 5.0 * centre + 2.0 * right_near) / 6.0
    part_three = (2.0 * centre + 5.0 * right_near - right_far) / 6.0
    smooth_one = 13.0 / 12.0 * (left_far - 2.0 * left_near + centre) ** 2 + 0.25 * (left_far - 4.0 * left_near + 3.0 * centre) ** 2
    smooth_two = 13.0 / 12.0 * (left_near - 2.0 * centre + right_near) ** 2 + 0.25 * (left_near - right_near) ** 2
    smooth_three = 13.0 / 12.0 * (centre - 2.0 * right_near + right_far) ** 2 + 0.25 * (3.0 * centre - 4.0 * right_near + right_far) ** 2
    weight_one = 0.1 / (WENO_EPSILON + smooth_one) ** 2
    weight_two = 0.6 / (WENO_EPSILON + smooth_two) ** 2
    weight_three = 0.3 / (WENO_EPSILON + smooth_three) ** 2
    return (weight_one * part_one + weight_two * part_two + weight_three * part_three) / (weight_one + weight_two + weight_three)

def weno_pair(padded, dimension):
    length = padded.shape[dimension] - 6
    deltas = jnp.diff(padded, axis=dimension)

    def window(offset):
        return lax.slice_in_dim(deltas, offset, offset + length, axis=dimension)
    minus_side = weno_blend(window(0), window(1), window(2), window(3), window(4))
    plus_side = weno_blend(window(5), window(4), window(3), window(2), window(1))
    return (minus_side, plus_side)

def upwind_square(minus_side, plus_side, positive):
    rising = jnp.maximum(jnp.maximum(minus_side, 0.0) ** 2, jnp.minimum(plus_side, 0.0) ** 2)
    falling = jnp.maximum(jnp.minimum(minus_side, 0.0) ** 2, jnp.maximum(plus_side, 0.0) ** 2)
    return jnp.where(positive, rising, falling)

def section_rate(values, sign_field, ghost_z, ghost_y, ghost_x):
    dim_count = values.ndim
    padded_z = jnp.concatenate([ghost_z[..., :3, :, :], values, ghost_z[..., 3:, :, :]], axis=dim_count - 3)
    padded_y = jnp.concatenate([ghost_y[..., :3, :], values, ghost_y[..., 3:, :]], axis=dim_count - 2)
    padded_x = jnp.concatenate([ghost_x[..., :3], values, ghost_x[..., 3:]], axis=dim_count - 1)
    positive = sign_field > 0
    minus_z, plus_z = weno_pair(padded_z, dim_count - 3)
    minus_y, plus_y = weno_pair(padded_y, dim_count - 2)
    minus_x, plus_x = weno_pair(padded_x, dim_count - 1)
    squared = upwind_square(minus_z, plus_z, positive) + upwind_square(minus_y, plus_y, positive) + upwind_square(minus_x, plus_x, positive)
    return -sign_field * (jnp.sqrt(squared) - 1.0)

def make_faces(values):
    face_z = jnp.concatenate([values[..., :3, :, :], values[..., -3:, :, :]], axis=3)
    face_y = jnp.concatenate([values[..., :3, :], values[..., -3:, :]], axis=4)
    face_x = jnp.concatenate([values[..., :3], values[..., -3:]], axis=5)
    return (face_z, face_y, face_x)

def shifted(source, dimension, upward):
    extent = source.shape[dimension]
    zero_rim = jnp.zeros_like(lax.slice_in_dim(source, 0, 1, axis=dimension))
    if upward:
        return jnp.concatenate([zero_rim, lax.slice_in_dim(source, 0, extent - 1, axis=dimension)], axis=dimension)
    return jnp.concatenate([lax.slice_in_dim(source, 1, extent, axis=dimension), zero_rim], axis=dimension)

def ghost_layers(face_z, face_y, face_x, active):
    is_live = active > 0
    results = []
    for dimension, faces in ((0, face_z), (1, face_y), (2, face_x)):
        rim_dim = dimension + 3
        from_low = shifted(is_live, dimension, True)[..., None, None, None]
        from_high = shifted(is_live, dimension, False)[..., None, None, None]
        low_faces = shifted(faces, dimension, True)
        high_faces = shifted(faces, dimension, False)
        lower = jnp.where(from_low, lax.slice_in_dim(low_faces, 3, 6, axis=rim_dim), lax.slice_in_dim(faces, 0, 1, axis=rim_dim))
        upper = jnp.where(from_high, lax.slice_in_dim(high_faces, 0, 3, axis=rim_dim), lax.slice_in_dim(faces, 5, 6, axis=rim_dim))
        results.append(jnp.concatenate([lower, upper], axis=rim_dim))
    return (results[0], results[1], results[2])

def evaluate(values, sign_field, active):
    face_z, face_y, face_x = make_faces(values)
    ghost_z, ghost_y, ghost_x = ghost_layers(face_z, face_y, face_x, active)
    flat = lambda array: array.reshape((-1,) + array.shape[3:])
    rates = lax.map(lambda member: section_rate(*member), (flat(values), flat(sign_field), flat(ghost_z), flat(ghost_y), flat(ghost_x)))
    return rates.reshape(values.shape)

def reference(level_set, active, destination):
    level_set = level_set.reshape(N_SLAB, N_COL, RX, BZ, BY, BX)
    sign_field = level_set / jnp.sqrt(level_set * level_set + 1.0)
    values = level_set
    for repeat in range(STEPS):
        rate_one = evaluate(values, sign_field, active)
        midway = values + TIME_STEP * rate_one
        rate_two = evaluate(midway, sign_field, active)
        values = 0.5 * values + 0.5 * (midway + TIME_STEP * rate_two)
    is_live = destination >= 0
    target_col = jnp.where(is_live, destination // W, N_COL).astype(jnp.int32)
    target_slot = jnp.where(is_live, destination % W, 0).astype(jnp.int32)
    slab_index = jnp.broadcast_to(jnp.arange(N_SLAB, dtype=jnp.int32)[:, None, None], destination.shape)
    placed = jnp.zeros((N_SLAB, N_COL, W, BZ, BY, BX), jnp.float32)
    placed = placed.at[slab_index, target_col, target_slot].set(values, mode='drop')
    return placed.reshape(N_SLAB, N_COL, W, BZ, BY * BX)
```

```python
import functools

import jax
import jax.numpy as jnp
from jax import lax
from jax.experimental import pallas as pl
from jax.experimental.pallas import tpu as pltpu
from jax.sharding import PartitionSpec as P

RX = 12
PAIRS = RX // 2
BZ = 16
W = 6
ROWS = 512
TIME_STEP = 0.3
MESH = pl.DeviceIdType.MESH


def reciprocal(x):
    return pl.reciprocal(x, approx=True)


def weno_squares(vals, sign):
    n = len(vals) - 6
    d = [vals[k + 1] - vals[k] for k in range(n + 5)]
    e = [d[k + 1] - d[k] for k in range(n + 4)]
    t = [e[k + 1] - e[k] for k in range(n + 3)]
    g = [t[k + 1] - t[k] for k in range(n + 2)]
    first, middle, last = {}, {}, {}
    for k in range(n + 3):
        a = e[k + 1] * t[k]
        b = e[k] * t[k]
        h = (a - b) * (2.0 / 3.0) + (e[k] * e[k + 1]) * 0.5 + 0.5e-6
        if k <= n:
            r = reciprocal(h + a)
            first[k] = r * r
        if 1 <= k <= n + 1:
            r = reciprocal(h)
            middle[k] = (r * r) * 6.0
        if k >= 2:
            r = reciprocal(h - b)
            last[k] = r * r
    first3 = {k: first[k] * 3.0 for k in range(1, n + 1)}
    last3 = {k: last[k] * 3.0 for k in range(2, n + 2)}
    g2 = [x + x for x in g]
    squares = []
    for i in range(n):
        centre = (vals[i + 4] - vals[i + 2]) * 3.0
        den = (first[i] + last3[i + 2]) + middle[i + 1]
        num = first[i] * g2[i] + last3[i + 2] * g[i + 1]
        minus = (centre - t[i + 1]) - num * reciprocal(den)
        den = (last[i + 3] + first3[i + 1]) + middle[i + 2]
        num = last[i + 3] * g2[i + 2] + first3[i + 1] * g[i + 1]
        plus = (t[i + 2] - centre) - num * reciprocal(den)
        w = jnp.maximum(jnp.maximum(minus * sign[i], plus * sign[i]), 0.0)
        squares.append(w * w)
    return squares


def sign_of(x):
    return jnp.where(x > 0, 1.0, -1.0)


def kernel(
    ns, nc,
    x_ref, act_ref, dst_ref, out_ref,
    cells, turned, zghost, yface, yghost, squares, xsq,
    flags, nflags, plan, plans, inverse, inverse_s,
    done, spread, collect, landed,
    zsend, zrecv, ysend, yrecv, fsend, frecv, dsend, drecv,
    p1send, p1recv, p2send, p2recv, isem,
):
    slab, col = lax.axis_index("slab"), lax.axis_index("col")
    lz = BZ // nc
    below, above = lax.rem(slab + ns - 1, ns), lax.rem(slab + 1, ns)
    left, right = lax.rem(col + nc - 1, nc), lax.rem(col + 1, nc)

    barrier = pltpu.get_barrier_semaphore()
    pl.semaphore_signal(barrier, inc=1, device_id=(below, col), device_id_type=MESH)
    pl.semaphore_signal(barrier, inc=1, device_id=(above, col), device_id_type=MESH)

    def greet(o, _):
        pl.semaphore_signal(
            barrier, inc=1, device_id=(slab, lax.rem(col + o, nc)), device_id_type=MESH
        )
        return 0

    lax.fori_loop(1, nc, greet, 0)

    lane = lax.broadcasted_iota(jnp.int32, (8, 128), 1)
    row = lax.broadcasted_iota(jnp.int32, (8, 128), 0)
    low_half = lane < 64

    def swap(v):
        return pltpu.roll(v, 64, 1)

    for p in range(PAIRS):
        flags[p : p + 1, :] = jnp.where(low_half, act_ref[2 * p], act_ref[2 * p + 1])[0:1]
    flags[PAIRS:8, :] = jnp.zeros((8 - PAIRS, 128), jnp.int32)
    mine = jnp.full((8, 128), -1, jnp.int32)
    for i in range(RX // 2, RX):
        mine = jnp.where(lane == i - RX // 2, dst_ref[i], mine)
    plan[...] = mine

    def pack_faces(st, p, z, vs):
        for k in range(3):
            yface[st, p, 0, k, pl.ds(z, 1), :] = vs[k][0:1]
            yface[st, p, 1, k, pl.ds(z, 1), :] = vs[5 + k][7:8]

    def turn(st, p, zz, vs):
        tile = jnp.concatenate(vs, axis=0).T
        turned[st, 2 * p, zz, 8:72, :] = tile[0:64]
        turned[st, 2 * p + 1, zz, 8:72, :] = tile[64:128]

    def convert(step, _):
        p = PAIRS - 1 - step

        def layer(zz, _):
            vs = []
            for q in range(2):
                z = 2 * zz + q
                base = ((zz // 4) * 32) * 8 + 2 * (zz % 4) + q
                for jj in range(4):
                    a = x_ref[pl.ds(2 * p * ROWS + base + 8 * jj, 8, stride=32), :]
                    b = x_ref[pl.ds((2 * p + 1) * ROWS + base + 8 * jj, 8, stride=32), :]
                    vs.append(jnp.where(low_half, a, swap(b)))
                    vs.append(jnp.where(low_half, swap(a), b))
                for j in range(8):
                    cells[0, p, z, j] = vs[8 * q + j]
                pack_faces(0, p, z, vs[8 * q :])
            turn(0, p, zz, vs)
            return 0

        lax.fori_loop(0, 8, layer, 0)
        return 0

    lax.fori_loop(0, PAIRS, convert, 0)

    pl.semaphore_wait(barrier, nc + 1)

    def face_copies(st, p):
        return (
            pltpu.make_async_remote_copy(
                src_ref=cells.at[st, p, 0:3], dst_ref=zghost.at[st, p, 1],
                send_sem=zsend.at[st, p, 1], recv_sem=zrecv.at[st, p, 1],
                device_id=(below, col), device_id_type=MESH,
            ),
            pltpu.make_async_remote_copy(
                src_ref=cells.at[st, p, 13:16], dst_ref=zghost.at[st, p, 0],
                send_sem=zsend.at[st, p, 0], recv_sem=zrecv.at[st, p, 0],
                device_id=(above, col), device_id_type=MESH,
            ),
            pltpu.make_async_remote_copy(
                src_ref=yface.at[st, p, 0], dst_ref=yghost.at[st, p, 1],
                send_sem=ysend.at[st, p, 1], recv_sem=yrecv.at[st, p, 1],
                device_id=(slab, left), device_id_type=MESH,
            ),
            pltpu.make_async_remote_copy(
                src_ref=yface.at[st, p, 1], dst_ref=yghost.at[st, p, 0],
                send_sem=ysend.at[st, p, 0], recv_sem=yrecv.at[st, p, 0],
                device_id=(slab, right), device_id_type=MESH,
            ),
        )

    def flag_copies():
        places = ((below, col), (above, col), (slab, left), (slab, right))
        return [
            pltpu.make_async_remote_copy(
                src_ref=flags, dst_ref=nflags.at[side],
                send_sem=fsend.at[side], recv_sem=frecv.at[side],
                device_id=place, device_id_type=MESH,
            )
            for side, place in zip((1, 0, 3, 2), places)
        ]

    def plan_copy(o):
        return pltpu.make_async_remote_copy(
            src_ref=plan, dst_ref=plans.at[col],
            send_sem=dsend.at[o - 1], recv_sem=drecv.at[o - 1],
            device_id=(slab, lax.rem(col + o, nc)), device_id_type=MESH,
        )

    def spread_copy(i, o):
        k = lax.rem(col + o, nc)
        return pltpu.make_async_remote_copy(
            src_ref=done.at[pl.ds(W + 2 * i, 2), pl.ds(k * lz, lz)],
            dst_ref=spread.at[pl.ds(col * W + 2 * i, 2)],
            send_sem=p1send.at[i, o - 1], recv_sem=p1recv.at[i, o - 1],
            device_id=(slab, k), device_id_type=MESH,
        )

    def collect_copy(o):
        k = lax.rem(col + o, nc)
        return pltpu.make_async_remote_copy(
            src_ref=collect.at[k], dst_ref=landed.at[col],
            send_sem=p2send.at[o - 1], recv_sem=p2recv.at[o - 1],
            device_id=(slab, k), device_id_type=MESH,
        )

    for copy in flag_copies():
        copy.start()

    def send_raw(step, _):
        for copy in face_copies(0, PAIRS - 1 - step):
            copy.start()
        return 0

    lax.fori_loop(0, PAIRS, send_raw, 0)

    def send_plan(o, _):
        plan_copy(o).start()
        return 0

    lax.fori_loop(1, nc, send_plan, 0)
    for copy in flag_copies():
        copy.wait_recv()
    has_below = jnp.where(slab > 0, 1, 0)
    has_above = jnp.where(slab < ns - 1, 1, 0)
    has_left = jnp.where(col > 0, 1, 0)
    has_right = jnp.where(col < nc - 1, 1, 0)

    def advance(st, p):
        keep = 0.5 * st.astype(jnp.float32)
        gain = 1.0 - keep
        speed = TIME_STEP * gain
        for copy in face_copies(st, p):
            copy.wait_recv()
        live_below = nflags[0, pl.ds(p, 1), :] * has_below > 0
        live_above = nflags[1, pl.ds(p, 1), :] * has_above > 0
        live_left = nflags[2, pl.ds(p, 1), :] * has_left > 0
        live_right = nflags[3, pl.ds(p, 1), :] * has_right > 0

        def along_z(j, _):
            core = [cells[st, p, z, j] for z in range(BZ)]
            lo = [jnp.where(live_below, zghost[st, p, 0, k, j], core[0]) for k in range(3)]
            hi = [jnp.where(live_above, zghost[st, p, 1, k, j], core[-1]) for k in range(3)]
            sign = [sign_of(cells[0, p, z, j]) for z in range(BZ)]
            for z, s in enumerate(weno_squares(lo + core + hi, sign)):
                squares[z, j] = s
            return 0

        lax.fori_loop(0, 8, along_z, 0)

        def edges(zz, _):
            for h in range(2):
                b = 2 * p + h
                before = jnp.where(b > 0, act_ref[jnp.maximum(b - 1, 0)], 0)
                after = jnp.where(b < RX - 1, act_ref[jnp.minimum(b + 1, RX - 1)], 0)
                lo = turned[st, jnp.maximum(b - 1, 0), zz, 64:72, :]
                hi = turned[st, jnp.minimum(b + 1, RX - 1), zz, 8:16, :]
                own_lo = turned[st, b, zz, 8:9, :]
                own_hi = turned[st, b, zz, 71:72, :]
                turned[st, b, zz, 0:8, :] = jnp.where(before > 0, lo, own_lo)
                turned[st, b, zz, 72:80, :] = jnp.where(after > 0, hi, own_hi)
            return 0

        lax.fori_loop(0, 8, edges, 0)

        def layers(zz, _):
            for h in range(2):
                b = 2 * p + h
                vals = [turned[st, b, zz, pl.ds(5 + j, 8, stride=8), :] for j in range(14)]
                sign = [
                    sign_of(turned[0, b, zz, pl.ds(8 + j, 8, stride=8), :]) for j in range(8)
                ]
                for j, s in enumerate(weno_squares(vals, sign)):
                    xsq[pl.ds(64 * h + j, 8, stride=8), :] = s
            across = xsq[...].T
            for q in range(2):
                z = 2 * zz + q
                core = [cells[st, p, z, j] for j in range(8)]
                base = [cells[0, p, z, j] for j in range(8)]
                lo, hi = [], []
                for k in range(3):
                    g_lo = jnp.where(live_left, yghost[st, p, 0, k, pl.ds(z, 1), :], core[0][0:1])
                    g_hi = jnp.where(live_right, yghost[st, p, 1, k, pl.ds(z, 1), :], core[7][7:8])
                    lo.append(jnp.where(row == 0, g_lo, pltpu.roll(core[5 + k], 1, 0)))
                    hi.append(jnp.where(row == 7, g_hi, pltpu.roll(core[k], 7, 0)))
                sign = [sign_of(v) for v in base]
                along_y = weno_squares(lo + core + hi, sign)
                for j in range(8):
                    v = base[j]
                    total = squares[z, j] + along_y[j] + across[64 * q + 8 * j : 64 * q + 8 * j + 8]
                    total = jnp.maximum(total, 1e-30)
                    root = total * lax.rsqrt(total)
                    field = v * lax.rsqrt(v * v + 1.0)
                    rate = field * (1.0 - root * (1.0 / 6.0))
                    cells[st + 1, p, z, j] = keep * v + gain * core[j] + speed * rate
            return 0

        lax.fori_loop(0, 8, layers, 0)

    def step(i, _):
        is_first = 1 - (i + 15) // 16
        is_last = (i + 5) // 16
        st = (i + 1) % 2 - is_first + is_last
        p = 4 - i // 2 + 2 * st + is_first - is_last

        @pl.when(i == 8)
        def _():
            exchange()

        advance(st, p)

        @pl.when(st == 0)
        def _():
            def layer(zz, _):
                vs = [cells[1, p, 2 * zz + q, j] for q in range(2) for j in range(8)]
                for q in range(2):
                    pack_faces(1, p, 2 * zz + q, vs[8 * q :])
                turn(1, p, zz, vs)
                return 0

            lax.fori_loop(0, 8, layer, 0)
            for copy in face_copies(1, p):
                copy.start()

        @pl.when(st == 1)
        def _():
            def layer(z, _):
                for jj in range(4):
                    a = cells[2, p, z, 2 * jj]
                    b = cells[2, p, z, 2 * jj + 1]
                    done[2 * p, z, jj] = jnp.where(low_half, a, swap(b))
                    done[2 * p + 1, z, jj] = jnp.where(low_half, swap(a), b)
                return 0

            lax.fori_loop(0, BZ, layer, 0)

            @pl.when(p >= PAIRS // 2)
            def _():
                def send(o, _):
                    spread_copy(p - PAIRS // 2, o).start()
                    return 0

                lax.fori_loop(1, nc, send, 0)

        return 0

    def exchange():
        def plan_in(o, _):
            plan_copy(o).wait_recv()
            return 0

        lax.fori_loop(1, nc, plan_in, 0)
        plans[col] = plan[...]
        place = lax.broadcasted_iota(jnp.int32, (128, 128), 0)
        wide = lax.broadcasted_iota(jnp.int32, (128, 128), 1)

        def match(s, found):
            target = plans[s][0:1]
            return found + jnp.where(target == place, wide + (s * W + 1), 0)

        found = lax.fori_loop(0, nc, match, jnp.zeros((128, 128), jnp.int32))
        for shift in (1, 2, 4, 8, 16, 32, 64):
            found = found + pltpu.roll(found, shift, 1)
        inverse[...] = found
        copy = pltpu.make_async_copy(inverse, inverse_s, isem)
        copy.start()
        copy.wait()
        for i in range(PAIRS // 2):
            def spread_in(o, _):
                spread_copy(i, o).wait_recv()
                return 0

            lax.fori_loop(1, nc, spread_in, 0)
        spread[pl.ds(col * W, W)] = done[W : 2 * W, pl.ds(col * lz, lz)]

        def hand(k, _):
            for w in range(W):
                e = jnp.clip(inverse_s[k * W + w, 0] - 1, 0, nc * W - 1)
                collect[k, w] = spread[e]
            return 0

        lax.fori_loop(0, nc, hand, 0)

        def send(o, _):
            collect_copy(o).start()
            return 0

        lax.fori_loop(1, nc, send, 0)
        landed[col] = collect[col]

    lax.fori_loop(0, 2 * PAIRS, step, 0)

    def landed_in(o, _):
        collect_copy(o).wait_recv()
        return 0

    lax.fori_loop(1, nc, landed_in, 0)

    def place_slot(w, _):
        slot = col * W + w
        moved = inverse_s[slot, 0]
        kept = 0
        for j in range(W):
            kept = kept + jnp.where(dst_ref[j] == slot, j + 1, 0)
        kept_at = jnp.clip(kept - 1, 0, W - 1)

        def layer(z, _):
            for jj in range(4):
                came = landed[z // lz, w, z % lz, jj]
                own = done[kept_at, z, jj]
                v = jnp.where(moved > 0, came, jnp.where(kept > 0, own, 0.0))
                start = w * ROWS + ((z // 8) * 32 + jj) * 8 + z % 8
                out_ref[pl.ds(start, 8, stride=32), :] = v
            return 0

        lax.fori_loop(0, BZ, layer, 0)
        return 0

    lax.fori_loop(0, W, place_slot, 0)

    for copy in flag_copies():
        copy.wait_send()

    def drain_faces(p, _):
        for st in range(2):
            for copy in face_copies(st, p):
                copy.wait_send()
        return 0

    lax.fori_loop(0, PAIRS, drain_faces, 0)

    def drain(o, _):
        plan_copy(o).wait_send()
        collect_copy(o).wait_send()
        for i in range(PAIRS // 2):
            spread_copy(i, o).wait_send()
        return 0

    lax.fori_loop(1, nc, drain, 0)


def shards(ns, nc, level_set, active, destination):
    lz = BZ // nc
    rows = (
        level_set.reshape(RX, 2, 8, 32, 128).transpose(0, 1, 3, 2, 4).reshape(RX * ROWS, 128)
    )
    dma = pltpu.SemaphoreType.DMA
    f32 = jnp.float32
    vmem = pl.BlockSpec(memory_space=pltpu.VMEM)
    smem = pl.BlockSpec(memory_space=pltpu.SMEM)
    result = pl.pallas_call(
        functools.partial(kernel, ns, nc),
        out_shape=jax.ShapeDtypeStruct((W * ROWS, 128), f32),
        in_specs=[vmem, smem, smem],
        out_specs=vmem,
        scratch_shapes=[
            pltpu.VMEM((3, PAIRS, BZ, 8, 8, 128), f32),
            pltpu.VMEM((2, RX, 8, 80, 128), f32),
            pltpu.VMEM((2, PAIRS, 2, 3, 8, 8, 128), f32),
            pltpu.VMEM((2, PAIRS, 2, 3, BZ, 128), f32),
            pltpu.VMEM((2, PAIRS, 2, 3, BZ, 128), f32),
            pltpu.VMEM((BZ, 8, 8, 128), f32),
            pltpu.VMEM((128, 128), f32),
            pltpu.VMEM((8, 128), jnp.int32),
            pltpu.VMEM((4, 8, 128), jnp.int32),
            pltpu.VMEM((8, 128), jnp.int32),
            pltpu.VMEM((nc, 8, 128), jnp.int32),
            pltpu.VMEM((128, 128), jnp.int32),
            pltpu.SMEM((128, 128), jnp.int32),
            pltpu.VMEM((RX, BZ, 4, 8, 128), f32),
            pltpu.VMEM((nc * W, lz, 4, 8, 128), f32),
            pltpu.VMEM((nc, W, lz, 4, 8, 128), f32),
            pltpu.VMEM((nc, W, lz, 4, 8, 128), f32),
            dma((2, PAIRS, 2)), dma((2, PAIRS, 2)), dma((2, PAIRS, 2)), dma((2, PAIRS, 2)),
            dma((4,)), dma((4,)), dma((nc - 1,)), dma((nc - 1,)),
            dma((PAIRS // 2, nc - 1)), dma((PAIRS // 2, nc - 1)),
            dma((nc - 1,)), dma((nc - 1,)), dma(()),
        ],
        compiler_params=pltpu.CompilerParams(
            collective_id=0, has_side_effects=True, vmem_limit_bytes=60 * 1024 * 1024
        ),
        cost_estimate=pl.CostEstimate(
            flops=300_000_000, bytes_accessed=5_000_000, transcendentals=0
        ),
    )(rows, active.reshape(RX), destination.reshape(RX))
    result = result.reshape(W, 2, 32, 8, 128).transpose(0, 1, 3, 2, 4)
    return result.reshape(1, 1, W, BZ, 4096)


def solution(mesh):
    ns, nc = mesh.shape["slab"], mesh.shape["col"]
    in_specs = (P("slab", "col", None, None, None), P("slab", "col", None), P("slab", "col", None))
    out_specs = P("slab", "col", None, None, None)
    return jax.shard_map(
        functools.partial(shards, ns, nc),
        mesh=mesh, in_specs=in_specs, out_specs=out_specs, check_vma=False,
    )
```

```python
import functools

import jax
import jax.numpy as jnp
from jax import lax
from jax.experimental import pallas as pl
from jax.experimental.pallas import tpu as pltpu
from jax.sharding import PartitionSpec as P

RX = 12
PAIRS = RX // 2
BZ = 16
W = 6
ROWS = 512
TIME_STEP = 0.3
MESH = pl.DeviceIdType.MESH


def reciprocal(x):
    return pl.reciprocal(x, approx=True)


def weno_squares(vals, sign):
    n = len(vals) - 6
    d = [vals[k + 1] - vals[k] for k in range(n + 5)]
    e = [d[k + 1] - d[k] for k in range(n + 4)]
    t = [e[k + 1] - e[k] for k in range(n + 3)]
    g = [t[k + 1] - t[k] for k in range(n + 2)]
    first, middle, last = {}, {}, {}
    for k in range(n + 3):
        a = e[k + 1] * t[k]
        b = e[k] * t[k]
        h = (a - b) * (2.0 / 3.0) + (e[k] * e[k + 1]) * 0.5 + 0.5e-6
        if k <= n:
            r = reciprocal(h + a)
            first[k] = r * r
        if 1 <= k <= n + 1:
            r = reciprocal(h)
            middle[k] = (r * r) * 6.0
        if k >= 2:
            r = reciprocal(h - b)
            last[k] = r * r
    first3 = {k: first[k] * 3.0 for k in range(1, n + 1)}
    last3 = {k: last[k] * 3.0 for k in range(2, n + 2)}
    g2 = [x + x for x in g]
    squares = []
    for i in range(n):
        centre = (vals[i + 4] - vals[i + 2]) * 3.0
        den = (first[i] + last3[i + 2]) + middle[i + 1]
        num = first[i] * g2[i] + last3[i + 2] * g[i + 1]
        minus = (centre - t[i + 1]) - num * reciprocal(den)
        den = (last[i + 3] + first3[i + 1]) + middle[i + 2]
        num = last[i + 3] * g2[i + 2] + first3[i + 1] * g[i + 1]
        plus = (t[i + 2] - centre) - num * reciprocal(den)
        w = jnp.maximum(jnp.maximum(minus * sign[i], plus * sign[i]), 0.0)
        squares.append(w * w)
    return squares


BIG = 1e30
LIMIT = 1e20
SHARE = 4


def kernel(
    ns, nc,
    x_ref, act_ref, dst_ref, out_ref,
    natural, cells, mids, turned, turned_mids, signs, turned_signs, pull,
    zghost, yface, yghost, squares, xsq,
    plan, plans, inverse, inverse_s,
    done, spread, collect, landed,
    zsend, zrecv, ysend, yrecv, dsend, drecv,
    p1send, p1recv, p2send, p2recv, isem, xsem,
):
    slab, col = lax.axis_index("slab"), lax.axis_index("col")
    lz = BZ // nc
    below, above = lax.rem(slab + ns - 1, ns), lax.rem(slab + 1, ns)
    left, right = lax.rem(col + nc - 1, nc), lax.rem(col + 1, nc)

    def load_pair(p):
        return pltpu.make_async_copy(
            x_ref.at[pl.ds(2 * p * ROWS, 2 * ROWS)],
            natural.at[pl.ds(2 * p * ROWS, 2 * ROWS)],
            xsem.at[p],
        )

    for p in reversed(range(PAIRS)):
        load_pair(p).start()

    barrier = pltpu.get_barrier_semaphore()
    pl.semaphore_signal(barrier, inc=1, device_id=(below, col), device_id_type=MESH)
    pl.semaphore_signal(barrier, inc=1, device_id=(above, col), device_id_type=MESH)

    def greet(o, _):
        pl.semaphore_signal(
            barrier, inc=1, device_id=(slab, lax.rem(col + o, nc)), device_id_type=MESH
        )
        return 0

    lax.fori_loop(1, nc, greet, 0)

    lane = lax.broadcasted_iota(jnp.int32, (8, 128), 1)
    row = lax.broadcasted_iota(jnp.int32, (8, 128), 0)
    low_half = lane < 64

    def swap(v):
        return pltpu.roll(v, 64, 1)

    columns = jnp.full((8, 128), -2, jnp.int32)
    slots = jnp.zeros((8, 128), jnp.int32)
    sends = 0
    for i in range(W):
        place = dst_ref[W + i]
        to = jnp.where(place >= 0, place // W, -1)
        leaves = jnp.where((place >= 0) & (to != col), 1, 0)
        sends = jnp.maximum(sends, leaves)
        columns = jnp.where(lane == i, jnp.where(leaves > 0, to, -2), columns)
        slots = jnp.where(lane == i, place % W, slots)
    plan[...] = jnp.where(row == 0, columns, jnp.where(row == 1, slots, sends))

    def pack_faces(st, p, z, vs):
        for k in range(3):
            yface[st, p, 0, k, pl.ds(z, 1), :] = vs[k][0:1]
            yface[st, p, 1, k, pl.ds(z, 1), :] = vs[5 + k][7:8]

    def convert(p):
        load_pair(p).wait()
        live_a, live_b = act_ref[2 * p] > 0, act_ref[2 * p + 1] > 0

        def layer(zz, _):
            vs = []
            for q in range(2):
                z = 2 * zz + q
                base = ((zz // 4) * 32) * 8 + 2 * (zz % 4) + q
                for jj in range(4):
                    a = natural[pl.ds(2 * p * ROWS + base + 8 * jj, 8, stride=32), :]
                    b = natural[pl.ds((2 * p + 1) * ROWS + base + 8 * jj, 8, stride=32), :]
                    a = jnp.where(live_a, a, BIG)
                    b = jnp.where(live_b, b, BIG)
                    vs.append(jnp.where(low_half, a, swap(b)))
                    vs.append(jnp.where(low_half, swap(a), b))
            tile = jnp.concatenate(vs, axis=0).T
            for q in range(2):
                z = 2 * zz + q
                for j in range(8):
                    v = vs[8 * q + j]
                    cells[p, z, j] = v
                    signs[p, z, j] = jnp.where(v > 0, 1.0, -1.0)
                pack_faces(0, p, z, vs[8 * q :])
            sign = jnp.where(tile > 0, 1.0, -1.0)
            turned[2 * p, zz, 8:72, :] = tile[0:64]
            turned[2 * p + 1, zz, 8:72, :] = tile[64:128]
            turned_signs[2 * p, zz] = sign[0:64]
            turned_signs[2 * p + 1, zz] = sign[64:128]
            return 0

        lax.fori_loop(0, 8, layer, 0, unroll=UNROLL_CONVERT)

    def face_copies(st, p):
        source = mids if st else cells
        return (
            pltpu.make_async_remote_copy(
                src_ref=source.at[p, 0:3], dst_ref=zghost.at[st, p, 1],
                send_sem=zsend.at[st, p, 1], recv_sem=zrecv.at[st, p, 1],
                device_id=(below, col), device_id_type=MESH,
            ),
            pltpu.make_async_remote_copy(
                src_ref=source.at[p, 13:16], dst_ref=zghost.at[st, p, 0],
                send_sem=zsend.at[st, p, 0], recv_sem=zrecv.at[st, p, 0],
                device_id=(above, col), device_id_type=MESH,
            ),
            pltpu.make_async_remote_copy(
                src_ref=yface.at[st, p, 0], dst_ref=yghost.at[st, p, 1],
                send_sem=ysend.at[st, p, 1], recv_sem=yrecv.at[st, p, 1],
                device_id=(slab, left), device_id_type=MESH,
            ),
            pltpu.make_async_remote_copy(
                src_ref=yface.at[st, p, 1], dst_ref=yghost.at[st, p, 0],
                send_sem=ysend.at[st, p, 0], recv_sem=yrecv.at[st, p, 0],
                device_id=(slab, right), device_id_type=MESH,
            ),
        )

    def plan_copy(o):
        return pltpu.make_async_remote_copy(
            src_ref=plan, dst_ref=plans.at[col], send_sem=dsend, recv_sem=drecv,
            device_id=(slab, lax.rem(col + o, nc)), device_id_type=MESH,
        )

    def spread_copy(i, o):
        k = lax.rem(col + o, nc)
        return pltpu.make_async_remote_copy(
            src_ref=done.at[pl.ds(W + 2 * i, 2), pl.ds(k * lz, lz)],
            dst_ref=spread.at[pl.ds(col * W + 2 * i, 2)],
            send_sem=p1send.at[i], recv_sem=p1recv.at[i],
            device_id=(slab, k), device_id_type=MESH,
        )

    def collect_copy(o):
        k = lax.rem(col + o, nc)
        return pltpu.make_async_remote_copy(
            src_ref=collect.at[k], dst_ref=landed.at[col], send_sem=p2send, recv_sem=p2recv,
            device_id=(slab, k), device_id_type=MESH,
        )

    def await_bytes(ref, sem):
        pltpu.make_async_copy(ref, ref, sem).wait()

    others = nc - 1
    convert(PAIRS - 1)
    pl.semaphore_wait(barrier, nc + 1)
    for copy in face_copies(0, PAIRS - 1):
        copy.start()

    def convert_next(i, _):
        p = PAIRS - 2 - i
        convert(p)
        for copy in face_copies(0, p):
            copy.start()
        return 0

    lax.fori_loop(0, PAIRS - 1, convert_next, 0)

    def send_plan(o, _):
        plan_copy(o).start()
        return 0

    lax.fori_loop(1, nc, send_plan, 0)
    lim_below = jnp.where(slab > 0, LIMIT, -1.0)
    lim_above = jnp.where(slab < ns - 1, LIMIT, -1.0)
    lim_left = jnp.where(col > 0, LIMIT, -1.0)
    lim_right = jnp.where(col < nc - 1, LIMIT, -1.0)

    def advance(st, p):
        now, turn = (mids, turned_mids) if st else (cells, turned)
        for copy in face_copies(st, p):
            copy.wait_recv()
        live_below = jnp.abs(zghost[st, p, 0, 0, 0, 0:1, :]) < lim_below
        live_above = jnp.abs(zghost[st, p, 1, 0, 0, 0:1, :]) < lim_above
        live_left = jnp.abs(yghost[st, p, 0, 0, 0:1, :]) < lim_left
        live_right = jnp.abs(yghost[st, p, 1, 0, 0:1, :]) < lim_right

        def along_z(j, _):
            core = [now[p, z, j] for z in range(BZ)]
            lo = [jnp.where(live_below, zghost[st, p, 0, k, j], core[0]) for k in range(3)]
            hi = [jnp.where(live_above, zghost[st, p, 1, k, j], core[-1]) for k in range(3)]
            sign = [signs[p, z, j] for z in range(BZ)]
            for z, s in enumerate(weno_squares(lo + core + hi, sign)):
                squares[z, j] = s
            return 0

        lax.fori_loop(0, 8, along_z, 0, unroll=UNROLL_Z)

        for h in range(2):
            b = 2 * p + h
            before = jnp.where(b > 0, act_ref[jnp.maximum(b - 1, 0)], 0) > 0
            after = jnp.where(b < RX - 1, act_ref[jnp.minimum(b + 1, RX - 1)], 0) > 0

            def edges(zz, _):
                lo = turn[jnp.maximum(b - 1, 0), zz, 64:72, :]
                hi = turn[jnp.minimum(b + 1, RX - 1), zz, 8:16, :]
                own_lo = turn[b, zz, 8:9, :]
                own_hi = turn[b, zz, 71:72, :]
                turn[b, zz, 0:8, :] = jnp.where(before, lo, own_lo)
                turn[b, zz, 72:80, :] = jnp.where(after, hi, own_hi)
                return 0

            lax.fori_loop(0, 8, edges, 0, unroll=UNROLL_EDGES)

        def layers(zz, _):
            for h in range(2):
                b = 2 * p + h
                vals = [turn[b, zz, pl.ds(5 + j, 8, stride=8), :] for j in range(14)]
                sign = [turned_signs[b, zz, pl.ds(j, 8, stride=8), :] for j in range(8)]
                for j, s in enumerate(weno_squares(vals, sign)):
                    xsq[zz % 2, pl.ds(64 * h + j, 8, stride=8), :] = s
            across = xsq[zz % 2].T
            result = []
            for q in range(2):
                z = 2 * zz + q
                core = [now[p, z, j] for j in range(8)]
                lo, hi = [], []
                for k in range(3):
                    g_lo = jnp.where(live_left, yghost[st, p, 0, k, pl.ds(z, 1), :], core[0][0:1])
                    g_hi = jnp.where(live_right, yghost[st, p, 1, k, pl.ds(z, 1), :], core[7][7:8])
                    lo.append(jnp.where(row == 0, g_lo, pltpu.roll(core[5 + k], 1, 0)))
                    hi.append(jnp.where(row == 7, g_hi, pltpu.roll(core[k], 7, 0)))
                sign = [signs[p, z, j] for j in range(8)]
                along_y = weno_squares(lo + core + hi, sign)
                for j in range(8):
                    total = squares[z, j] + along_y[j] + across[64 * q + 8 * j : 64 * q + 8 * j + 8]
                    total = jnp.maximum(total, 1e-30)
                    gain = 1.0 - (total * lax.rsqrt(total)) * (1.0 / 6.0)
                    if st == 0:
                        v = core[j]
                        field = (v * TIME_STEP) * lax.rsqrt(v * v + 1.0)
                        pull[p, z, j] = field
                        result.append(v + field * gain)
                    else:
                        result.append(0.5 * (cells[p, z, j] + core[j] + pull[p, z, j] * gain))
            if st == 0:
                for q in range(2):
                    for j in range(8):
                        mids[p, 2 * zz + q, j] = result[8 * q + j]
                    pack_faces(1, p, 2 * zz + q, result[8 * q :])
                tile = jnp.concatenate(result, axis=0).T
                turned_mids[2 * p, zz, 8:72, :] = tile[0:64]
                turned_mids[2 * p + 1, zz, 8:72, :] = tile[64:128]
            else:
                for q in range(2):
                    for jj in range(4):
                        a, b = result[8 * q + 2 * jj], result[8 * q + 2 * jj + 1]
                        done[2 * p, 2 * zz + q, jj] = jnp.where(low_half, a, swap(b))
                        done[2 * p + 1, 2 * zz + q, jj] = jnp.where(low_half, swap(a), b)
            return 0

        lax.fori_loop(0, 8, layers, 0, unroll=UNROLL_LAYERS)

    def step(i, _):
        is_first = 1 - (i + 15) // 16
        is_last = (i + 5) // 16
        st = (i + 1) % 2 - is_first + is_last
        p = 4 - i // 2 + 2 * st + is_first - is_last

        @pl.when(i == EXCHANGE_AT)
        def _():
            exchange()

        @pl.when(st == 0)
        def _():
            advance(0, p)
            for copy in face_copies(1, p):
                copy.start()

        @pl.when(st == 1)
        def _():
            advance(1, p)

            @pl.when(p >= PAIRS // 2)
            def _():
                def send(o, _):
                    spread_copy(p - PAIRS // 2, o).start()
                    return 0

                lax.fori_loop(1, nc, send, 0)

        return 0

    def exchange():
        await_bytes(plans.at[pl.ds(0, others)], drecv)
        plans[col] = plan[...]
        place = lax.broadcasted_iota(jnp.int32, (nc * SHARE, 128), 0)
        wide = lax.broadcasted_iota(jnp.int32, (1, 128), 1)

        def match(s, carry):
            found, rank = carry
            key = plans[s, 0:1, :] * SHARE + rank
            code = (wide + (s * W + 1)) * 8 + plans[s, 1:2, :]
            return found + jnp.where(key == place, code, 0), rank + plans[s, 2:3, :]

        found, _ = lax.fori_loop(
            0, nc, match,
            (jnp.zeros((nc * SHARE, 128), jnp.int32), jnp.zeros((1, 128), jnp.int32)),
        )
        for shift in (1, 2, 4, 8, 16, 32, 64):
            found = found + pltpu.roll(found, shift, 1)
        inverse[...] = found
        copy = pltpu.make_async_copy(inverse, inverse_s, isem)
        copy.start()
        copy.wait()
        for i in range(PAIRS // 2):
            await_bytes(spread.at[pl.ds(0, 2 * others)], p1recv.at[i])
        spread[pl.ds(col * W, W)] = done[W : 2 * W, pl.ds(col * lz, lz)]

        def hand(k, _):
            for c in range(SHARE):
                e = jnp.clip(inverse_s[k * SHARE + c, 0] // 8 - 1, 0, nc * W - 1)
                collect[k, c] = spread[e]
            return 0

        lax.fori_loop(0, nc, hand, 0)

        def send(o, _):
            collect_copy(o).start()
            return 0

        lax.fori_loop(1, nc, send, 0)
        landed[col] = collect[col]

    lax.fori_loop(0, 2 * PAIRS, step, 0)

    await_bytes(landed.at[pl.ds(0, others)], p2recv)

    def place_slot(w, _):
        moved = 0
        for c in range(SHARE):
            code = inverse_s[col * SHARE + c, 0]
            moved = moved + jnp.where((code > 0) & (code % 8 == w), c + 1, 0)
        kept = 0
        for j in range(RX):
            kept = kept + jnp.where(dst_ref[j] == col * W + w, j + 1, 0)
        moved_at = jnp.clip(moved - 1, 0, SHARE - 1)
        kept_at = jnp.clip(kept - 1, 0, RX - 1)

        def layer(z, _):
            for jj in range(4):
                came = landed[z // lz, moved_at, z % lz, jj]
                own = done[kept_at, z, jj]
                v = jnp.where(moved > 0, came, jnp.where(kept > 0, own, 0.0))
                start = w * ROWS + ((z // 8) * 32 + jj) * 8 + z % 8
                out_ref[pl.ds(start, 8, stride=32), :] = v
            return 0

        lax.fori_loop(0, BZ, layer, 0, unroll=4)
        return 0

    lax.fori_loop(0, W, place_slot, 0)

    def drain_faces(p, _):
        for st in range(2):
            for copy in face_copies(st, p):
                copy.wait_send()
        return 0

    lax.fori_loop(0, PAIRS, drain_faces, 0)
    await_bytes(plans.at[pl.ds(0, others)], dsend)
    for i in range(PAIRS // 2):
        await_bytes(spread.at[pl.ds(0, 2 * others)], p1send.at[i])
    await_bytes(landed.at[pl.ds(0, others)], p2send)


UNROLL_CONVERT = 4
UNROLL_Z = 2
UNROLL_EDGES = 4
UNROLL_LAYERS = 4
EXCHANGE_AT = 8


def shards(ns, nc, level_set, active, destination):
    lz = BZ // nc
    rows = (
        level_set.reshape(RX, 2, 8, 32, 128).transpose(0, 1, 3, 2, 4).reshape(RX * ROWS, 128)
    )
    dma = pltpu.SemaphoreType.DMA
    f32 = jnp.float32
    vmem = pl.BlockSpec(memory_space=pltpu.VMEM)
    smem = pl.BlockSpec(memory_space=pltpu.SMEM)
    result = pl.pallas_call(
        functools.partial(kernel, ns, nc),
        out_shape=jax.ShapeDtypeStruct((W * ROWS, 128), f32),
        in_specs=[pl.BlockSpec(memory_space=pl.ANY), smem, smem],
        out_specs=vmem,
        scratch_shapes=[
            pltpu.VMEM((RX * ROWS, 128), f32),
            pltpu.VMEM((PAIRS, BZ, 8, 8, 128), f32),
            pltpu.VMEM((PAIRS, BZ, 8, 8, 128), f32),
            pltpu.VMEM((RX, 8, 80, 128), f32),
            pltpu.VMEM((RX, 8, 80, 128), f32),
            pltpu.VMEM((PAIRS, BZ, 8, 8, 128), f32),
            pltpu.VMEM((RX, 8, 64, 128), f32),
            pltpu.VMEM((PAIRS, BZ, 8, 8, 128), f32),
            pltpu.VMEM((2, PAIRS, 2, 3, 8, 8, 128), f32),
            pltpu.VMEM((2, PAIRS, 2, 3, BZ, 128), f32),
            pltpu.VMEM((2, PAIRS, 2, 3, BZ, 128), f32),
            pltpu.VMEM((BZ, 8, 8, 128), f32),
            pltpu.VMEM((2, 128, 128), f32),
            pltpu.VMEM((8, 128), jnp.int32),
            pltpu.VMEM((nc, 8, 128), jnp.int32),
            pltpu.VMEM((nc * SHARE, 128), jnp.int32),
            pltpu.SMEM((nc * SHARE, 128), jnp.int32),
            pltpu.VMEM((RX, BZ, 4, 8, 128), f32),
            pltpu.VMEM((nc * W, lz, 4, 8, 128), f32),
            pltpu.VMEM((nc, SHARE, lz, 4, 8, 128), f32),
            pltpu.VMEM((nc, SHARE, lz, 4, 8, 128), f32),
            dma((2, PAIRS, 2)), dma((2, PAIRS, 2)), dma((2, PAIRS, 2)), dma((2, PAIRS, 2)),
            dma(()), dma(()), dma((PAIRS // 2,)), dma((PAIRS // 2,)),
            dma(()), dma(()), dma(()), dma((PAIRS,)),
        ],
        compiler_params=pltpu.CompilerParams(
            collective_id=0, has_side_effects=True, vmem_limit_bytes=60 * 1024 * 1024
        ),
        cost_estimate=pl.CostEstimate(
            flops=300_000_000, bytes_accessed=5_000_000, transcendentals=0
        ),
    )(rows, active.reshape(RX), destination.reshape(RX))
    result = result.reshape(W, 2, 32, 8, 128).transpose(0, 1, 3, 2, 4)
    return result.reshape(1, 1, W, BZ, 4096)


def solution(mesh):
    ns, nc = mesh.shape["slab"], mesh.shape["col"]
    in_specs = (P("slab", "col", None, None, None), P("slab", "col", None), P("slab", "col", None))
    out_specs = P("slab", "col", None, None, None)
    return jax.shard_map(
        functools.partial(shards, ns, nc),
        mesh=mesh, in_specs=in_specs, out_specs=out_specs, check_vma=False,
    )
```

```python
import functools

import jax
import jax.numpy as jnp
from jax import lax
from jax.experimental import pallas as pl
from jax.experimental.pallas import tpu as pltpu
from jax.sharding import PartitionSpec as P

RX = 12
PAIRS = RX // 2
BZ = 16
W = 6
ROWS = 512
TIME_STEP = 0.3
MESH = pl.DeviceIdType.MESH


def reciprocal(x):
    return pl.reciprocal(x, approx=True)


def weno_squares(vals, sign):
    n = len(vals) - 6
    d = [vals[k + 1] - vals[k] for k in range(n + 5)]
    e = [d[k + 1] - d[k] for k in range(n + 4)]
    t = [e[k + 1] - e[k] for k in range(n + 3)]
    g = [t[k + 1] - t[k] for k in range(n + 2)]
    first, middle, last = {}, {}, {}
    for k in range(n + 3):
        a = e[k + 1] * t[k]
        b = e[k] * t[k]
        h = (a - b) * (2.0 / 3.0) + (e[k] * e[k + 1]) * 0.5 + 0.5e-6
        if k <= n:
            r = reciprocal(h + a)
            first[k] = r * r
        if 1 <= k <= n + 1:
            r = reciprocal(h)
            middle[k] = (r * r) * 6.0
        if k >= 2:
            r = reciprocal(h - b)
            last[k] = r * r
    first3 = {k: first[k] * 3.0 for k in range(1, n + 1)}
    last3 = {k: last[k] * 3.0 for k in range(2, n + 2)}
    g2 = [x + x for x in g]
    squares = []
    for i in range(n):
        centre = (vals[i + 4] - vals[i + 2]) * 3.0
        den = (first[i] + last3[i + 2]) + middle[i + 1]
        num = first[i] * g2[i] + last3[i + 2] * g[i + 1]
        minus = (centre - t[i + 1]) - num * reciprocal(den)
        den = (last[i + 3] + first3[i + 1]) + middle[i + 2]
        num = last[i + 3] * g2[i + 2] + first3[i + 1] * g[i + 1]
        plus = (t[i + 2] - centre) - num * reciprocal(den)
        w = jnp.maximum(jnp.maximum(minus * sign[i], plus * sign[i]), 0.0)
        squares.append(w * w)
    return squares


BIG = 1e30
LIMIT = 1e20
SHARE = 4


def home_layer(k):
    x, z = k // 4, k % 4
    return 8 * ((x + z) % 2) + 2 * x + z // 2


def kernel(
    ns, nc,
    x_ref, act_ref, dst_ref, out_ref,
    natural, cells, mids, turned, turned_mids, signs, turned_signs, pull,
    zghost, yface, yghost, squares, across, xsq,
    plan, plans, inverse, inverse_s,
    leaving, spread, collect, landed,
    zsend, zrecv, ysend, yrecv, dsend, drecv,
    p1send, p1recv, p2send, p2recv, isem, xsem,
):
    slab, col = lax.axis_index("slab"), lax.axis_index("col")
    below, above = lax.rem(slab + ns - 1, ns), lax.rem(slab + 1, ns)
    left, right = lax.rem(col + nc - 1, nc), lax.rem(col + 1, nc)
    own_layer, own_x = home_layer(col), col // 4

    def load_pair(p):
        return pltpu.make_async_copy(
            x_ref.at[pl.ds(2 * p * ROWS, 2 * ROWS)],
            natural.at[pl.ds(2 * p * ROWS, 2 * ROWS)],
            xsem.at[p],
        )

    for p in reversed(range(PAIRS)):
        load_pair(p).start()

    barrier = pltpu.get_barrier_semaphore()
    pl.semaphore_signal(barrier, inc=1, device_id=(below, col), device_id_type=MESH)
    pl.semaphore_signal(barrier, inc=1, device_id=(above, col), device_id_type=MESH)

    def greet(o, _):
        pl.semaphore_signal(
            barrier, inc=1, device_id=(slab, lax.rem(col + o, nc)), device_id_type=MESH
        )
        return 0

    lax.fori_loop(1, nc, greet, 0)

    lane = lax.broadcasted_iota(jnp.int32, (8, 128), 1)
    row = lax.broadcasted_iota(jnp.int32, (8, 128), 0)
    low_half = lane < 64

    def swap(v):
        return pltpu.roll(v, 64, 1)

    columns = jnp.full((8, 128), -2, jnp.int32)
    slots = jnp.zeros((8, 128), jnp.int32)
    sends = 0
    for i in range(W):
        place = dst_ref[W + i]
        to = jnp.where(place >= 0, place // W, -1)
        leaves = jnp.where((place >= 0) & (to != col), 1, 0)
        sends = jnp.maximum(sends, leaves)
        columns = jnp.where(lane == i, jnp.where(leaves > 0, to, -2), columns)
        slots = jnp.where(lane == i, place % W, slots)
    plan[...] = jnp.where(row == 0, columns, jnp.where(row == 1, slots, sends))

    def pack_faces(st, p, z, vs):
        for k in range(3):
            yface[st, p, 0, k, pl.ds(z, 1), :] = vs[k][0:1]
            yface[st, p, 1, k, pl.ds(z, 1), :] = vs[5 + k][7:8]

    def convert(p):
        load_pair(p).wait()
        live_a, live_b = act_ref[2 * p] > 0, act_ref[2 * p + 1] > 0

        def layer(zh, zq, _):
            zz = 4 * zh + zq
            vs = []
            for q in range(2):
                base = zh * 256 + 2 * zq + q
                for jj in range(4):
                    a = natural[pl.ds(2 * p * ROWS + base + 8 * jj, 8, stride=32), :]
                    b = natural[pl.ds((2 * p + 1) * ROWS + base + 8 * jj, 8, stride=32), :]
                    a = jnp.where(live_a, a, BIG)
                    b = jnp.where(live_b, b, BIG)
                    vs.append(jnp.where(low_half, a, swap(b)))
                    vs.append(jnp.where(low_half, swap(a), b))
            tile = jnp.concatenate(vs, axis=0).T
            for q in range(2):
                z = 2 * zz + q
                for j in range(8):
                    v = vs[8 * q + j]
                    cells[p, z, j] = v
                    signs[p, z, j] = jnp.where(v > 0, 1.0, -1.0)
                pack_faces(0, p, z, vs[8 * q :])
            sign = jnp.where(tile > 0, 1.0, -1.0)
            turned[2 * p, zz, 8:72, :] = tile[0:64]
            turned[2 * p + 1, zz, 8:72, :] = tile[64:128]
            turned_signs[2 * p, zz] = sign[0:64]
            turned_signs[2 * p + 1, zz] = sign[64:128]
            return 0

        for zh in range(2):
            lax.fori_loop(0, 4, functools.partial(layer, zh), 0, unroll=UNROLL_CONVERT)

    def face_copies(st, p):
        source = mids if st else cells
        return (
            pltpu.make_async_remote_copy(
                src_ref=source.at[p, 0:3], dst_ref=zghost.at[st, p, 1],
                send_sem=zsend.at[st, p, 1], recv_sem=zrecv.at[st, p, 1],
                device_id=(below, col), device_id_type=MESH,
            ),
            pltpu.make_async_remote_copy(
                src_ref=source.at[p, 13:16], dst_ref=zghost.at[st, p, 0],
                send_sem=zsend.at[st, p, 0], recv_sem=zrecv.at[st, p, 0],
                device_id=(above, col), device_id_type=MESH,
            ),
            pltpu.make_async_remote_copy(
                src_ref=yface.at[st, p, 0], dst_ref=yghost.at[st, p, 1],
                send_sem=ysend.at[st, p, 1], recv_sem=yrecv.at[st, p, 1],
                device_id=(slab, left), device_id_type=MESH,
            ),
            pltpu.make_async_remote_copy(
                src_ref=yface.at[st, p, 1], dst_ref=yghost.at[st, p, 0],
                send_sem=ysend.at[st, p, 0], recv_sem=yrecv.at[st, p, 0],
                device_id=(slab, right), device_id_type=MESH,
            ),
        )

    def plan_copy(o):
        return pltpu.make_async_remote_copy(
            src_ref=plan, dst_ref=plans.at[col], send_sem=dsend, recv_sem=drecv,
            device_id=(slab, lax.rem(col + o, nc)), device_id_type=MESH,
        )

    def spread_copy(i, layer, home):
        return pltpu.make_async_remote_copy(
            src_ref=leaving.at[layer, pl.ds(W + 2 * i, 2)],
            dst_ref=spread.at[pl.ds(col * W + 2 * i, 2)],
            send_sem=p1send.at[i], recv_sem=p1recv.at[i],
            device_id=(slab, home), device_id_type=MESH,
        )

    def collect_copy(o):
        k = lax.rem(col + o, nc)
        return pltpu.make_async_remote_copy(
            src_ref=collect.at[k], dst_ref=landed.at[own_layer], send_sem=p2send, recv_sem=p2recv,
            device_id=(slab, k), device_id_type=MESH,
        )

    def await_bytes(ref, sem):
        pltpu.make_async_copy(ref, ref, sem).wait()

    others = nc - 1
    def send_plan(o, _):
        plan_copy(o).start()
        return 0

    lim_below = jnp.where(slab > 0, LIMIT, -1.0)
    lim_above = jnp.where(slab < ns - 1, LIMIT, -1.0)
    lim_left = jnp.where(col > 0, LIMIT, -1.0)
    lim_right = jnp.where(col < nc - 1, LIMIT, -1.0)

    def along_x(st, p):
        turn = turned_mids if st else turned
        for h in range(2):
            b = 2 * p + h
            before = jnp.where(b > 0, act_ref[jnp.maximum(b - 1, 0)], 0) > 0
            after = jnp.where(b < RX - 1, act_ref[jnp.minimum(b + 1, RX - 1)], 0) > 0

            def edges(zz, _):
                lo = turn[jnp.maximum(b - 1, 0), zz, 64:72, :]
                hi = turn[jnp.minimum(b + 1, RX - 1), zz, 8:16, :]
                own_lo = turn[b, zz, 8:9, :]
                own_hi = turn[b, zz, 71:72, :]
                turn[b, zz, 0:8, :] = jnp.where(before, lo, own_lo)
                turn[b, zz, 72:80, :] = jnp.where(after, hi, own_hi)
                return 0

            lax.fori_loop(0, 8, edges, 0, unroll=UNROLL_EDGES)

        def strip(zz, _):
            for h in range(2):
                b = 2 * p + h
                vals = [turn[b, zz, pl.ds(5 + j, 8, stride=8), :] for j in range(14)]
                sign = [turned_signs[b, zz, pl.ds(j, 8, stride=8), :] for j in range(8)]
                for j, s in enumerate(weno_squares(vals, sign)):
                    xsq[zz, pl.ds(64 * h + j, 8, stride=8), :] = s
            across[p, zz] = xsq[zz].T
            return 0

        lax.fori_loop(0, 8, strip, 0, unroll=UNROLL_X)

    def advance(st, p):
        now = mids if st else cells
        for copy in face_copies(st, p):
            copy.wait_recv()
        live_below = jnp.abs(zghost[st, p, 0, 0, 0, 0:1, :]) < lim_below
        live_above = jnp.abs(zghost[st, p, 1, 0, 0, 0:1, :]) < lim_above
        live_left = jnp.abs(yghost[st, p, 0, 0, 0:1, :]) < lim_left
        live_right = jnp.abs(yghost[st, p, 1, 0, 0:1, :]) < lim_right

        def along_z(j, _):
            core = [now[p, z, j] for z in range(BZ)]
            lo = [jnp.where(live_below, zghost[st, p, 0, k, j], core[0]) for k in range(3)]
            hi = [jnp.where(live_above, zghost[st, p, 1, k, j], core[-1]) for k in range(3)]
            sign = [signs[p, z, j] for z in range(BZ)]
            for z, s in enumerate(weno_squares(lo + core + hi, sign)):
                squares[z, j] = s
            return 0

        lax.fori_loop(0, 8, along_z, 0, unroll=UNROLL_Z)

        def layers(zz, _):
            result = []
            for q in range(2):
                z = 2 * zz + q
                core = [now[p, z, j] for j in range(8)]
                lo, hi = [], []
                for k in range(3):
                    g_lo = jnp.where(live_left, yghost[st, p, 0, k, pl.ds(z, 1), :], core[0][0:1])
                    g_hi = jnp.where(live_right, yghost[st, p, 1, k, pl.ds(z, 1), :], core[7][7:8])
                    lo.append(jnp.where(row == 0, g_lo, pltpu.roll(core[5 + k], 1, 0)))
                    hi.append(jnp.where(row == 7, g_hi, pltpu.roll(core[k], 7, 0)))
                sign = [signs[p, z, j] for j in range(8)]
                along_y = weno_squares(lo + core + hi, sign)
                for j in range(8):
                    total = squares[z, j] + along_y[j] + across[p, zz, 64 * q + 8 * j : 64 * q + 8 * j + 8, :]
                    total = jnp.maximum(total, 1e-30)
                    gain = 1.0 - (total * lax.rsqrt(total)) * (1.0 / 6.0)
                    if st == 0:
                        v = core[j]
                        field = (v * TIME_STEP) * lax.rsqrt(v * v + 1.0)
                        pull[p, z, j] = field
                        result.append(v + field * gain)
                    else:
                        result.append(0.5 * (cells[p, z, j] + core[j] + pull[p, z, j] * gain))
            if st == 0:
                for q in range(2):
                    for j in range(8):
                        mids[p, 2 * zz + q, j] = result[8 * q + j]
                    pack_faces(1, p, 2 * zz + q, result[8 * q :])
                tile = jnp.concatenate(result, axis=0).T
                turned_mids[2 * p, zz, 8:72, :] = tile[0:64]
                turned_mids[2 * p + 1, zz, 8:72, :] = tile[64:128]
            else:
                for q in range(2):
                    for jj in range(4):
                        a, b = result[8 * q + 2 * jj], result[8 * q + 2 * jj + 1]
                        a, b = jnp.where(low_half, a, swap(b)), jnp.where(low_half, swap(a), b)
                        leaving[2 * zz + q, 2 * p, jj] = a
                        leaving[2 * zz + q, 2 * p + 1, jj] = b
            return 0

        for half in range(2):
            lax.fori_loop(4 * half, 4 * half + 4, layers, 0, unroll=UNROLL_LAYERS)
            if st == 1:

                @pl.when(p >= PAIRS // 2)
                def _():
                    def send(o, _):
                        x = lax.rem(own_x + o, 4)
                        for b in range(2):
                            layer = 8 * half + 2 * x + b
                            home = 4 * x + 2 * b + lax.rem(x + half, 2)

                            @pl.when(home != col)
                            def _():
                                spread_copy(p - PAIRS // 2, layer, home).start()

                        return 0

                    lax.fori_loop(0, 4, send, 0)

    def step(i, _):
        is_first, late, final = 1 - (i + 15) // 16, (i + 9) // 16, (i + 7) // 16
        st = (1 - late) * ((i + 1) % 2 - is_first) + final
        p = (1 - late) * (4 - i // 2 + 2 * st + is_first) + late * (8 - i + 3 * final)

        @pl.when(st == 0)
        def _():
            @pl.when(p < EARLY)
            def _():
                along_x(0, p)

            @pl.when(i == 3)
            def _():
                lax.fori_loop(4, PAIRS, send_raw, 0)
                tables()

            advance(0, p)
            for copy in face_copies(1, p):
                copy.start()

        @pl.when(st == 1)
        def _():
            @pl.when(i == EXCHANGE_AT)
            def _():
                exchange()

            along_x(1, p)
            advance(1, p)

        return 0

    def tables():
        await_bytes(plans.at[pl.ds(0, others)], drecv)
        plans[col] = plan[...]
        place = lax.broadcasted_iota(jnp.int32, (nc * SHARE, 128), 0)
        wide = lax.broadcasted_iota(jnp.int32, (1, 128), 1)

        def match(s, carry):
            found, rank = carry
            key = plans[s, 0:1, :] * SHARE + rank
            code = (wide + (s * W + 1)) * 8 + plans[s, 1:2, :]
            return found + jnp.where(key == place, code, 0), rank + plans[s, 2:3, :]

        found, _ = lax.fori_loop(
            0, nc, match,
            (jnp.zeros((nc * SHARE, 128), jnp.int32), jnp.zeros((1, 128), jnp.int32)),
        )
        for shift in (1, 2, 4, 8, 16, 32, 64):
            found = found + pltpu.roll(found, shift, 1)
        inverse[...] = found
        copy = pltpu.make_async_copy(inverse, inverse_s, isem)
        copy.start()
        copy.wait()

    def exchange():
        for i in range(PAIRS // 2):
            await_bytes(spread.at[pl.ds(0, 2 * others)], p1recv.at[i])
        spread[pl.ds(col * W, W)] = leaving[own_layer, W : 2 * W]

        def hand(k, _):
            for c in range(SHARE):
                e = jnp.clip(inverse_s[k * SHARE + c, 0] // 8 - 1, 0, nc * W - 1)
                collect[k, c] = spread[e]
            return 0

        lax.fori_loop(0, nc, hand, 0, unroll=2)

        def send(o, _):
            collect_copy(o).start()
            return 0

        lax.fori_loop(1, nc, send, 0)
        landed[own_layer] = collect[col]

    def convert_next(i, _):
        convert(PAIRS - 1 - i)
        return 0

    lax.fori_loop(0, PAIRS, convert_next, 0)
    def send_raw(i, _):
        for copy in face_copies(0, PAIRS - 1 - i):
            copy.start()
        return 0

    def early(i, _):
        @pl.when(i == 0)
        def _():
            pl.semaphore_wait(barrier, nc + 1)
            lax.fori_loop(0, 2, send_raw, 0)

        along_x(0, PAIRS - 1 - i)

        @pl.when(i == 1)
        def _():
            lax.fori_loop(2, 4, send_raw, 0)
            lax.fori_loop(1, nc, send_plan, 0)

        return 0

    lax.fori_loop(0, PAIRS - EARLY, early, 0)
    lax.fori_loop(0, 2 * PAIRS, step, 0)

    await_bytes(landed.at[pl.ds(0, others)], p2recv)

    def place_slot(w, _):
        kept = 0
        for j in range(RX):
            kept = kept + jnp.where(dst_ref[j] == col * W + w, j + 1, 0)
        kept_at = jnp.clip(kept - 1, 0, RX - 1)
        moved = 0
        for c in range(SHARE):
            code = inverse_s[col * SHARE + c, 0]
            moved = moved + jnp.where((code > 0) & (code % 8 == w), c + 1, 0)
        moved_at = jnp.clip(moved - 1, 0, SHARE - 1)

        def layer(z, _):
            for zh in range(2):
                for jj in range(4):
                    came = landed[8 * zh + z, moved_at, jj]
                    own = leaving[8 * zh + z, kept_at, jj]
                    v = jnp.where(moved > 0, came, jnp.where(kept > 0, own, 0.0))
                    out_ref[pl.ds(w * ROWS + zh * 256 + jj * 8 + z, 8, stride=32), :] = v
            return 0

        lax.fori_loop(0, 8, layer, 0, unroll=UNROLL_PLACE)
        return 0

    lax.fori_loop(0, W, place_slot, 0)

    def drain_faces(p, _):
        for st in range(2):
            for copy in face_copies(st, p):
                copy.wait_send()
        return 0

    lax.fori_loop(0, PAIRS, drain_faces, 0)
    await_bytes(plans.at[pl.ds(0, others)], dsend)
    for i in range(PAIRS // 2):
        await_bytes(spread.at[pl.ds(0, 2 * others)], p1send.at[i])
    await_bytes(landed.at[pl.ds(0, others)], p2send)


UNROLL_CONVERT = 4
UNROLL_Z = 4
UNROLL_EDGES = 4
UNROLL_LAYERS = 4
EXCHANGE_AT = 9
UNROLL_X = 8
UNROLL_PLACE = 2
EARLY = 3


def shards(ns, nc, level_set, active, destination):
    rows = (
        level_set.reshape(RX, 2, 8, 32, 128).transpose(0, 1, 3, 2, 4).reshape(RX * ROWS, 128)
    )
    dma = pltpu.SemaphoreType.DMA
    f32 = jnp.float32
    vmem = pl.BlockSpec(memory_space=pltpu.VMEM)
    smem = pl.BlockSpec(memory_space=pltpu.SMEM)
    result = pl.pallas_call(
        functools.partial(kernel, ns, nc),
        out_shape=jax.ShapeDtypeStruct((W * ROWS, 128), f32),
        in_specs=[pl.BlockSpec(memory_space=pl.ANY), smem, smem],
        out_specs=vmem,
        scratch_shapes=[
            pltpu.VMEM((RX * ROWS, 128), f32),
            pltpu.VMEM((PAIRS, BZ, 8, 8, 128), f32),
            pltpu.VMEM((PAIRS, BZ, 8, 8, 128), f32),
            pltpu.VMEM((RX, 8, 80, 128), f32),
            pltpu.VMEM((RX, 8, 80, 128), f32),
            pltpu.VMEM((PAIRS, BZ, 8, 8, 128), f32),
            pltpu.VMEM((RX, 8, 64, 128), f32),
            pltpu.VMEM((PAIRS, BZ, 8, 8, 128), f32),
            pltpu.VMEM((2, PAIRS, 2, 3, 8, 8, 128), f32),
            pltpu.VMEM((2, PAIRS, 2, 3, BZ, 128), f32),
            pltpu.VMEM((2, PAIRS, 2, 3, BZ, 128), f32),
            pltpu.VMEM((BZ, 8, 8, 128), f32),
            pltpu.VMEM((PAIRS, 8, 128, 128), f32),
            pltpu.VMEM((8, 128, 128), f32),
            pltpu.VMEM((8, 128), jnp.int32),
            pltpu.VMEM((nc, 8, 128), jnp.int32),
            pltpu.VMEM((nc * SHARE, 128), jnp.int32),
            pltpu.SMEM((nc * SHARE, 128), jnp.int32),
            pltpu.VMEM((BZ, RX, 4, 8, 128), f32),
            pltpu.VMEM((nc * W, 4, 8, 128), f32),
            pltpu.VMEM((nc, SHARE, 4, 8, 128), f32),
            pltpu.VMEM((nc, SHARE, 4, 8, 128), f32),
            dma((2, PAIRS, 2)), dma((2, PAIRS, 2)), dma((2, PAIRS, 2)), dma((2, PAIRS, 2)),
            dma(()), dma(()), dma((PAIRS // 2,)), dma((PAIRS // 2,)),
            dma(()), dma(()), dma(()), dma((PAIRS,)),
        ],
        compiler_params=pltpu.CompilerParams(
            collective_id=0, has_side_effects=True, vmem_limit_bytes=60 * 1024 * 1024
        ),
        cost_estimate=pl.CostEstimate(
            flops=300_000_000, bytes_accessed=5_000_000, transcendentals=0
        ),
    )(rows, active.reshape(RX), destination.reshape(RX))
    result = result.reshape(W, 2, 32, 8, 128).transpose(0, 1, 3, 2, 4)
    return result.reshape(1, 1, W, BZ, 4096)


def solution(mesh):
    ns, nc = mesh.shape["slab"], mesh.shape["col"]
    in_specs = (P("slab", "col", None, None, None), P("slab", "col", None), P("slab", "col", None))
    out_specs = P("slab", "col", None, None, None)
    return jax.shard_map(
        functools.partial(shards, ns, nc),
        mesh=mesh, in_specs=in_specs, out_specs=out_specs, check_vma=False,
    )
```

```python
import functools

import jax
import jax.numpy as jnp
from jax import lax
from jax.experimental import pallas as pl
from jax.experimental.pallas import tpu as pltpu
from jax.sharding import PartitionSpec as P

RX = 12
PAIRS = RX // 2
BZ = 16
W = 6
ROWS = 512
TIME_STEP = 0.3
MESH = pl.DeviceIdType.MESH


def reciprocal(x):
    return pl.reciprocal(x, approx=True)


def weno_squares(vals, sign):
    n = len(vals) - 6
    d = [vals[k + 1] - vals[k] for k in range(n + 5)]
    e = [d[k + 1] - d[k] for k in range(n + 4)]
    t = [e[k + 1] - e[k] for k in range(n + 3)]
    g = [t[k + 1] - t[k] for k in range(n + 2)]
    first, middle, last = {}, {}, {}
    for k in range(n + 3):
        a = e[k + 1] * t[k]
        b = e[k] * t[k]
        h = (a - b) * (2.0 / 3.0) + (e[k] * e[k + 1]) * 0.5 + 0.5e-6
        if k <= n:
            r = reciprocal(h + a)
            first[k] = r * r
        if 1 <= k <= n + 1:
            r = reciprocal(h)
            middle[k] = (r * r) * 6.0
        if k >= 2:
            r = reciprocal(h - b)
            last[k] = r * r
    first3 = {k: first[k] * 3.0 for k in range(1, n + 1)}
    last3 = {k: last[k] * 3.0 for k in range(2, n + 2)}
    g2 = [x + x for x in g]
    squares = []
    for i in range(n):
        centre = (vals[i + 4] - vals[i + 2]) * 3.0
        den = (first[i] + last3[i + 2]) + middle[i + 1]
        num = first[i] * g2[i] + last3[i + 2] * g[i + 1]
        minus = (centre - t[i + 1]) - num * reciprocal(den)
        den = (last[i + 3] + first3[i + 1]) + middle[i + 2]
        num = last[i + 3] * g2[i + 2] + first3[i + 1] * g[i + 1]
        plus = (t[i + 2] - centre) - num * reciprocal(den)
        w = jnp.maximum(jnp.maximum(minus * sign[i], plus * sign[i]), 0.0)
        squares.append(w * w)
    return squares


BIG = 1e30
LIMIT = 1e20
SHARE = 4


def home_layer(k):
    x, z = k // 4, k % 4
    return 8 * ((x + z) % 2) + 2 * x + z // 2


def kernel(
    ns, nc,
    x_ref, act_ref, dst_ref, out_ref,
    natural, cells, mids, turned, turned_mids, signs, turned_signs, pull,
    zghost, yface, yghost, squares, across, xsq,
    plan, plans, inverse, inverse_s,
    leaving, spread, collect, landed,
    zsend, zrecv, ysend, yrecv, dsend, drecv,
    p1send, p1recv, p2send, p2recv, isem, xsem,
):
    slab, col = lax.axis_index("slab"), lax.axis_index("col")
    below, above = lax.rem(slab + ns - 1, ns), lax.rem(slab + 1, ns)
    left, right = lax.rem(col + nc - 1, nc), lax.rem(col + 1, nc)
    own_layer, own_x = home_layer(col), col // 4

    def load_pair(p):
        return pltpu.make_async_copy(
            x_ref.at[pl.ds(2 * p * ROWS, 2 * ROWS)],
            natural.at[pl.ds(2 * p * ROWS, 2 * ROWS)],
            xsem.at[p],
        )

    for p in reversed(range(PAIRS)):
        load_pair(p).start()

    barrier = pltpu.get_barrier_semaphore()
    pl.semaphore_signal(barrier, inc=1, device_id=(below, col), device_id_type=MESH)
    pl.semaphore_signal(barrier, inc=1, device_id=(above, col), device_id_type=MESH)

    def greet(o, _):
        pl.semaphore_signal(
            barrier, inc=1, device_id=(slab, lax.rem(col + o, nc)), device_id_type=MESH
        )
        return 0

    lax.fori_loop(1, nc, greet, 0)

    lane = lax.broadcasted_iota(jnp.int32, (8, 128), 1)
    row = lax.broadcasted_iota(jnp.int32, (8, 128), 0)
    low_half = lane < 64

    def swap(v):
        return pltpu.roll(v, 64, 1)

    columns = jnp.full((8, 128), -2, jnp.int32)
    slots = jnp.zeros((8, 128), jnp.int32)
    sends = 0
    for i in range(W):
        place = dst_ref[W + i]
        to = jnp.where(place >= 0, place // W, -1)
        leaves = jnp.where((place >= 0) & (to != col), 1, 0)
        sends = jnp.maximum(sends, leaves)
        columns = jnp.where(lane == i, jnp.where(leaves > 0, to, -2), columns)
        slots = jnp.where(lane == i, place % W, slots)
    plan[...] = jnp.where(row == 0, columns, jnp.where(row == 1, slots, sends))

    def pack_faces(st, p, z, vs):
        for k in range(3):
            yface[st, p, 0, k, pl.ds(z, 1), :] = vs[k][0:1]
            yface[st, p, 1, k, pl.ds(z, 1), :] = vs[5 + k][7:8]

    def convert(p):
        load_pair(p).wait()
        live_a, live_b = act_ref[2 * p] > 0, act_ref[2 * p + 1] > 0

        def layer(zh, zq, _):
            zz = 4 * zh + zq
            vs = []
            for q in range(2):
                base = zh * 256 + 2 * zq + q
                for jj in range(4):
                    a = natural[pl.ds(2 * p * ROWS + base + 8 * jj, 8, stride=32), :]
                    b = natural[pl.ds((2 * p + 1) * ROWS + base + 8 * jj, 8, stride=32), :]
                    a = jnp.where(live_a, a, BIG)
                    b = jnp.where(live_b, b, BIG)
                    vs.append(jnp.where(low_half, a, swap(b)))
                    vs.append(jnp.where(low_half, swap(a), b))
            tile = jnp.concatenate(vs, axis=0).T
            for q in range(2):
                z = 2 * zz + q
                for j in range(8):
                    v = vs[8 * q + j]
                    cells[p, z, j] = v
                    signs[p, z, j] = jnp.where(v > 0, 1.0, -1.0)
                pack_faces(0, p, z, vs[8 * q :])
            sign = jnp.where(tile > 0, 1.0, -1.0)
            turned[2 * p, zz, 8:72, :] = tile[0:64]
            turned[2 * p + 1, zz, 8:72, :] = tile[64:128]
            turned_signs[2 * p, zz] = sign[0:64]
            turned_signs[2 * p + 1, zz] = sign[64:128]
            return 0

        for zh in range(2):
            lax.fori_loop(0, 4, functools.partial(layer, zh), 0, unroll=UNROLL_CONVERT)

    def face_copies(st, p):
        source = mids if st else cells
        return (
            pltpu.make_async_remote_copy(
                src_ref=source.at[p, 0:3], dst_ref=zghost.at[st, p, 1],
                send_sem=zsend.at[st, p, 1], recv_sem=zrecv.at[st, p, 1],
                device_id=(below, col), device_id_type=MESH,
            ),
            pltpu.make_async_remote_copy(
                src_ref=source.at[p, 13:16], dst_ref=zghost.at[st, p, 0],
                send_sem=zsend.at[st, p, 0], recv_sem=zrecv.at[st, p, 0],
                device_id=(above, col), device_id_type=MESH,
            ),
            pltpu.make_async_remote_copy(
                src_ref=yface.at[st, p, 0], dst_ref=yghost.at[st, p, 1],
                send_sem=ysend.at[st, p, 1], recv_sem=yrecv.at[st, p, 1],
                device_id=(slab, left), device_id_type=MESH,
            ),
            pltpu.make_async_remote_copy(
                src_ref=yface.at[st, p, 1], dst_ref=yghost.at[st, p, 0],
                send_sem=ysend.at[st, p, 0], recv_sem=yrecv.at[st, p, 0],
                device_id=(slab, right), device_id_type=MESH,
            ),
        )

    def plan_copy(o):
        return pltpu.make_async_remote_copy(
            src_ref=plan, dst_ref=plans.at[col], send_sem=dsend, recv_sem=drecv,
            device_id=(slab, lax.rem(col + o, nc)), device_id_type=MESH,
        )

    def spread_copy(i, layer, home):
        return pltpu.make_async_remote_copy(
            src_ref=leaving.at[layer, pl.ds(W + 2 * i, 2)],
            dst_ref=spread.at[pl.ds(col * W + 2 * i, 2)],
            send_sem=p1send.at[i], recv_sem=p1recv.at[i],
            device_id=(slab, home), device_id_type=MESH,
        )

    def collect_copy(o):
        k = lax.rem(col + o, nc)
        return pltpu.make_async_remote_copy(
            src_ref=collect.at[k], dst_ref=landed.at[own_layer], send_sem=p2send, recv_sem=p2recv,
            device_id=(slab, k), device_id_type=MESH,
        )

    def await_bytes(ref, sem):
        pltpu.make_async_copy(ref, ref, sem).wait()

    others = nc - 1
    def send_plan(o, _):
        plan_copy(o).start()
        return 0

    lim_below = jnp.where(slab > 0, LIMIT, -1.0)
    lim_above = jnp.where(slab < ns - 1, LIMIT, -1.0)
    lim_left = jnp.where(col > 0, LIMIT, -1.0)
    lim_right = jnp.where(col < nc - 1, LIMIT, -1.0)

    def along_x(st, p):
        turn = turned_mids if st else turned
        for h in range(2):
            b = 2 * p + h
            before = jnp.where(b > 0, act_ref[jnp.maximum(b - 1, 0)], 0) > 0
            after = jnp.where(b < RX - 1, act_ref[jnp.minimum(b + 1, RX - 1)], 0) > 0

            def edges(zz, _):
                lo = turn[jnp.maximum(b - 1, 0), zz, 64:72, :]
                hi = turn[jnp.minimum(b + 1, RX - 1), zz, 8:16, :]
                own_lo = turn[b, zz, 8:9, :]
                own_hi = turn[b, zz, 71:72, :]
                turn[b, zz, 0:8, :] = jnp.where(before, lo, own_lo)
                turn[b, zz, 72:80, :] = jnp.where(after, hi, own_hi)
                return 0

            lax.fori_loop(0, 8, edges, 0, unroll=UNROLL_EDGES)

        def strip(zz, _):
            for h in range(2):
                b = 2 * p + h
                vals = [turn[b, zz, pl.ds(5 + j, 8, stride=8), :] for j in range(14)]
                sign = [turned_signs[b, zz, pl.ds(j, 8, stride=8), :] for j in range(8)]
                for j, s in enumerate(weno_squares(vals, sign)):
                    xsq[zz, pl.ds(64 * h + j, 8, stride=8), :] = s
            across[p, zz] = xsq[zz].T
            return 0

        lax.fori_loop(0, 8, strip, 0, unroll=UNROLL_X)

    def advance(st, p):
        now = mids if st else cells
        for copy in face_copies(st, p):
            copy.wait_recv()
        live_below = jnp.abs(zghost[st, p, 0, 0, 0, 0:1, :]) < lim_below
        live_above = jnp.abs(zghost[st, p, 1, 0, 0, 0:1, :]) < lim_above
        live_left = jnp.abs(yghost[st, p, 0, 0, 0:1, :]) < lim_left
        live_right = jnp.abs(yghost[st, p, 1, 0, 0:1, :]) < lim_right

        def along_z(j, _):
            core = [now[p, z, j] for z in range(BZ)]
            lo = [jnp.where(live_below, zghost[st, p, 0, k, j], core[0]) for k in range(3)]
            hi = [jnp.where(live_above, zghost[st, p, 1, k, j], core[-1]) for k in range(3)]
            sign = [signs[p, z, j] for z in range(BZ)]
            for z, s in enumerate(weno_squares(lo + core + hi, sign)):
                squares[z, j] = s
            return 0

        lax.fori_loop(0, 8, along_z, 0, unroll=UNROLL_Z)

        def layers(zz, _):
            result = []
            for q in range(2):
                z = 2 * zz + q
                core = [now[p, z, j] for j in range(8)]
                lo, hi = [], []
                for k in range(3):
                    g_lo = jnp.where(live_left, yghost[st, p, 0, k, pl.ds(z, 1), :], core[0][0:1])
                    g_hi = jnp.where(live_right, yghost[st, p, 1, k, pl.ds(z, 1), :], core[7][7:8])
                    lo.append(jnp.where(row == 0, g_lo, pltpu.roll(core[5 + k], 1, 0)))
                    hi.append(jnp.where(row == 7, g_hi, pltpu.roll(core[k], 7, 0)))
                sign = [signs[p, z, j] for j in range(8)]
                along_y = weno_squares(lo + core + hi, sign)
                for j in range(8):
                    total = squares[z, j] + along_y[j] + across[p, zz, 64 * q + 8 * j : 64 * q + 8 * j + 8, :]
                    total = jnp.maximum(total, 1e-30)
                    gain = 1.0 - (total * lax.rsqrt(total)) * (1.0 / 6.0)
                    if st == 0:
                        v = core[j]
                        field = (v * TIME_STEP) * lax.rsqrt(v * v + 1.0)
                        pull[p, z, j] = field
                        result.append(v + field * gain)
                    else:
                        result.append(0.5 * (cells[p, z, j] + core[j] + pull[p, z, j] * gain))
            if st == 0:
                for q in range(2):
                    for j in range(8):
                        mids[p, 2 * zz + q, j] = result[8 * q + j]
                    pack_faces(1, p, 2 * zz + q, result[8 * q :])
                tile = jnp.concatenate(result, axis=0).T
                turned_mids[2 * p, zz, 8:72, :] = tile[0:64]
                turned_mids[2 * p + 1, zz, 8:72, :] = tile[64:128]
            else:
                for q in range(2):
                    for jj in range(4):
                        a, b = result[8 * q + 2 * jj], result[8 * q + 2 * jj + 1]
                        a, b = jnp.where(low_half, a, swap(b)), jnp.where(low_half, swap(a), b)
                        leaving[2 * zz + q, 2 * p, jj] = a
                        leaving[2 * zz + q, 2 * p + 1, jj] = b
            return 0

        for half in range(2):
            lax.fori_loop(4 * half, 4 * half + 4, layers, 0, unroll=UNROLL_LAYERS)
            if st == 1:

                @pl.when(p >= PAIRS // 2)
                def _():
                    def send(o, _):
                        x = lax.rem(own_x + o, 4)
                        for b in range(2):
                            layer = 8 * half + 2 * x + b
                            home = 4 * x + 2 * b + lax.rem(x + half, 2)

                            @pl.when(home != col)
                            def _():
                                spread_copy(p - PAIRS // 2, layer, home).start()

                        return 0

                    lax.fori_loop(0, 4, send, 0)

    def step(i, _):
        is_first, late, final = 1 - (i + 15) // 16, (i + 9) // 16, (i + 7) // 16
        st = (1 - late) * ((i + 1) % 2 - is_first) + final
        p = (1 - late) * (4 - i // 2 + 2 * st + is_first) + late * (8 - i + 3 * final)

        @pl.when(st == 0)
        def _():
            @pl.when(p < EARLY)
            def _():
                along_x(0, p)

            @pl.when(i == 3)
            def _():
                lax.fori_loop(4, PAIRS, send_raw, 0)
                tables()

            advance(0, p)
            for copy in face_copies(1, p):
                copy.start()

        @pl.when(st == 1)
        def _():
            @pl.when(i == EXCHANGE_AT)
            def _():
                exchange()

            along_x(1, p)
            advance(1, p)

        return 0

    def tables():
        await_bytes(plans.at[pl.ds(0, others)], drecv)
        plans[col] = plan[...]
        place = lax.broadcasted_iota(jnp.int32, (nc * SHARE, 128), 0)
        wide = lax.broadcasted_iota(jnp.int32, (1, 128), 1)

        def match(s, carry):
            found, rank = carry
            key = plans[s, 0:1, :] * SHARE + rank
            code = (wide + (s * W + 1)) * 8 + plans[s, 1:2, :]
            return found + jnp.where(key == place, code, 0), rank + plans[s, 2:3, :]

        found, _ = lax.fori_loop(
            0, nc, match,
            (jnp.zeros((nc * SHARE, 128), jnp.int32), jnp.zeros((1, 128), jnp.int32)),
        )
        for shift in (1, 2, 4, 8, 16, 32, 64):
            found = found + pltpu.roll(found, shift, 1)
        inverse[...] = found
        copy = pltpu.make_async_copy(inverse, inverse_s, isem)
        copy.start()
        copy.wait()

    def exchange():
        for i in range(PAIRS // 2):
            await_bytes(spread.at[pl.ds(0, 2 * others)], p1recv.at[i])
        spread[pl.ds(col * W, W)] = leaving[own_layer, W : 2 * W]

        def hand(k, _):
            for c in range(SHARE):
                e = jnp.clip(inverse_s[k * SHARE + c, 0] // 8 - 1, 0, nc * W - 1)
                collect[k, c] = spread[e]
            return 0

        lax.fori_loop(0, nc, hand, 0, unroll=4)

        def send(o, _):
            collect_copy(o).start()
            return 0

        lax.fori_loop(1, nc, send, 0)
        landed[own_layer] = collect[col]

    def convert_next(i, _):
        convert(PAIRS - 1 - i)
        return 0

    lax.fori_loop(0, PAIRS, convert_next, 0)
    def send_raw(i, _):
        for copy in face_copies(0, PAIRS - 1 - i):
            copy.start()
        return 0

    def early(i, _):
        @pl.when(i == 0)
        def _():
            pl.semaphore_wait(barrier, nc + 1)
            lax.fori_loop(0, 2, send_raw, 0)

        along_x(0, PAIRS - 1 - i)

        @pl.when(i == 1)
        def _():
            lax.fori_loop(2, 4, send_raw, 0)
            lax.fori_loop(1, nc, send_plan, 0)

        return 0

    lax.fori_loop(0, PAIRS - EARLY, early, 0)
    lax.fori_loop(0, 2 * PAIRS, step, 0)

    await_bytes(landed.at[pl.ds(0, others)], p2recv)

    def place_slot(w, _):
        kept = 0
        for j in range(RX):
            kept = kept + jnp.where(dst_ref[j] == col * W + w, j + 1, 0)
        kept_at = jnp.clip(kept - 1, 0, RX - 1)
        moved = 0
        for c in range(SHARE):
            code = inverse_s[col * SHARE + c, 0]
            moved = moved + jnp.where((code > 0) & (code % 8 == w), c + 1, 0)
        moved_at = jnp.clip(moved - 1, 0, SHARE - 1)

        def layer(z, _):
            for zh in range(2):
                for jj in range(4):
                    came = landed[8 * zh + z, moved_at, jj]
                    own = leaving[8 * zh + z, kept_at, jj]
                    v = jnp.where(moved > 0, came, jnp.where(kept > 0, own, 0.0))
                    out_ref[pl.ds(w * ROWS + zh * 256 + jj * 8 + z, 8, stride=32), :] = v
            return 0

        lax.fori_loop(0, 8, layer, 0, unroll=UNROLL_PLACE)
        return 0

    lax.fori_loop(0, W, place_slot, 0)

    def drain_faces(p, _):
        for st in range(2):
            for copy in face_copies(st, p):
                copy.wait_send()
        return 0

    lax.fori_loop(0, PAIRS, drain_faces, 0)
    await_bytes(plans.at[pl.ds(0, others)], dsend)
    for i in range(PAIRS // 2):
        await_bytes(spread.at[pl.ds(0, 2 * others)], p1send.at[i])
    await_bytes(landed.at[pl.ds(0, others)], p2send)


UNROLL_CONVERT = 4
UNROLL_Z = 4
UNROLL_EDGES = 8
UNROLL_LAYERS = 4
EXCHANGE_AT = 9
UNROLL_X = 8
UNROLL_PLACE = 8
EARLY = 3


def shards(ns, nc, level_set, active, destination):
    rows = (
        level_set.reshape(RX, 2, 8, 32, 128).transpose(0, 1, 3, 2, 4).reshape(RX * ROWS, 128)
    )
    dma = pltpu.SemaphoreType.DMA
    f32 = jnp.float32
    vmem = pl.BlockSpec(memory_space=pltpu.VMEM)
    smem = pl.BlockSpec(memory_space=pltpu.SMEM)
    result = pl.pallas_call(
        functools.partial(kernel, ns, nc),
        out_shape=jax.ShapeDtypeStruct((W * ROWS, 128), f32),
        in_specs=[pl.BlockSpec(memory_space=pl.ANY), smem, smem],
        out_specs=vmem,
        scratch_shapes=[
            pltpu.VMEM((RX * ROWS, 128), f32),
            pltpu.VMEM((PAIRS, BZ, 8, 8, 128), f32),
            pltpu.VMEM((PAIRS, BZ, 8, 8, 128), f32),
            pltpu.VMEM((RX, 8, 80, 128), f32),
            pltpu.VMEM((RX, 8, 80, 128), f32),
            pltpu.VMEM((PAIRS, BZ, 8, 8, 128), f32),
            pltpu.VMEM((RX, 8, 64, 128), f32),
            pltpu.VMEM((PAIRS, BZ, 8, 8, 128), f32),
            pltpu.VMEM((2, PAIRS, 2, 3, 8, 8, 128), f32),
            pltpu.VMEM((2, PAIRS, 2, 3, BZ, 128), f32),
            pltpu.VMEM((2, PAIRS, 2, 3, BZ, 128), f32),
            pltpu.VMEM((BZ, 8, 8, 128), f32),
            pltpu.VMEM((PAIRS, 8, 128, 128), f32),
            pltpu.VMEM((8, 128, 128), f32),
            pltpu.VMEM((8, 128), jnp.int32),
            pltpu.VMEM((nc, 8, 128), jnp.int32),
            pltpu.VMEM((nc * SHARE, 128), jnp.int32),
            pltpu.SMEM((nc * SHARE, 128), jnp.int32),
            pltpu.VMEM((BZ, RX, 4, 8, 128), f32),
            pltpu.VMEM((nc * W, 4, 8, 128), f32),
            pltpu.VMEM((nc, SHARE, 4, 8, 128), f32),
            pltpu.VMEM((nc, SHARE, 4, 8, 128), f32),
            dma((2, PAIRS, 2)), dma((2, PAIRS, 2)), dma((2, PAIRS, 2)), dma((2, PAIRS, 2)),
            dma(()), dma(()), dma((PAIRS // 2,)), dma((PAIRS // 2,)),
            dma(()), dma(()), dma(()), dma((PAIRS,)),
        ],
        compiler_params=pltpu.CompilerParams(
            collective_id=0, has_side_effects=True, vmem_limit_bytes=60 * 1024 * 1024
        ),
        cost_estimate=pl.CostEstimate(
            flops=300_000_000, bytes_accessed=5_000_000, transcendentals=0
        ),
    )(rows, active.reshape(RX), destination.reshape(RX))
    result = result.reshape(W, 2, 32, 8, 128).transpose(0, 1, 3, 2, 4)
    return result.reshape(1, 1, W, BZ, 4096)


def solution(mesh):
    ns, nc = mesh.shape["slab"], mesh.shape["col"]
    in_specs = (P("slab", "col", None, None, None), P("slab", "col", None), P("slab", "col", None))
    out_specs = P("slab", "col", None, None, None)
    return jax.shard_map(
        functools.partial(shards, ns, nc),
        mesh=mesh, in_specs=in_specs, out_specs=out_specs, check_vma=False,
    )
```
